32 devices in a mesh: rep: 4 (over x, core), shard: 8 (over z, y).
Axes of the slice: x: 2, y: 2, z: 4, core: 2. Of those that a mesh axis runs over, the one named last changes fastest.
Arguments:
- tokens: bfloat16 [32768, 1024], P(('rep', 'shard')), may hold values from -6 to 6
- cotangent: bfloat16 [32768, 1024], P(('rep', 'shard')), may hold values from -6 to 6
- qkv_weight: float32 [1024, 2048], P('shard'), may hold values from -0.1875 to 0.1875
- out_weight: float32 [1024, 1024], P('shard'), may hold values from -1 to 1
- gateup_weight: float32 [1024, 9216], P('shard'), may hold values from -0.1875 to 0.1875
- down_weight: float32 [4608, 1024], P('shard'), may hold values from -0.09375 to 0.09375
- norm_gains: float32 [2176], P('shard'), may hold values from 0.5 to 1.5
- avg_qkv: float32 [1024, 2048], P('shard'), may hold values from -160 to 160
- avg_out: float32 [1024, 1024], P('shard'), may hold values from -16 to 16
- avg_gateup: float32 [1024, 9216], P('shard'), may hold values from -64 to 64
- avg_down: float32 [4608, 1024], P('shard'), may hold values from -64 to 64
- avg_gains: float32 [2176], P('shard'), may hold values from -256 to 256
- sq_qkv: float32 [1024, 2048], P('shard'), may hold values from 65.536 to 262.144
- sq_out: float32 [1024, 1024], P('shard'), may hold values from 0.65536 to 2.62144
- sq_gateup: float32 [1024, 9216], P('shard'), may hold values from 9.8304 to 39.3216
- sq_down: float32 [4608, 1024], P('shard'), may hold values from 9.8304 to 39.3216
- sq_gains: float32 [2176], P('shard'), may hold values from 131.072 to 524.288
Outputs:
- block_out: bfloat16 [32768, 1024], P(('rep', 'shard'))
- grad_tokens: bfloat16 [32768, 1024], P(('rep', 'shard'))
- grad_qkv: float32 [1024, 2048], P('shard')
- grad_out: float32 [1024, 1024], P('shard')
- grad_gateup: float32 [1024, 9216], P('shard')
- grad_down: float32 [4608, 1024], P('shard')
- grad_gains: float32 [2176], P('shard')
- new_qkv: float32 [1024, 2048], P('shard')
- new_out: float32 [1024, 1024], P('shard')
- new_gateup: float32 [1024, 9216], P('shard')
- new_down: float32 [4608, 1024], P('shard')
- new_gains: float32 [2176], P('shard')
- avgnew_qkv: float32 [1024, 2048], P('shard')
- avgnew_out: float32 [1024, 1024], P('shard')
- avgnew_gateup: float32 [1024, 9216], P('shard')
- avgnew_down: float32 [4608, 1024], P('shard')
- avgnew_gains: float32 [2176], P('shard')
- sqnew_qkv: float32 [1024, 2048], P('shard')
- sqnew_out: float32 [1024, 1024], P('shard')
- sqnew_gateup: float32 [1024, 9216], P('shard')
- sqnew_down: float32 [4608, 1024], P('shard')
- sqnew_gains: float32 [2176], P('shard')
The draws below stay inside these ranges and needn't reach their ends.
All inputs are finite; a program needn't handle non-finite values.
Results may differ from the reference program's by a relative error of at most 0.018.
Values may be sent and summed in bfloat16 or wider, within the bound.
A program may use at most 384 MiB of HBM per device.

```python
import math
import jax
import jax.numpy as jnp
from jax import lax

D = 1024
HEADS = 16
KV_HEADS = 8
HEAD_DIM = 64
FF = 4608
LEN = 1024
STEP = 10
GAINS = 2176
TOKENS = 32768


def steps_of(stream_key, dims, shards, smallest, high):
    factor_of = 1.0
    for position, shards_of in shards:
        draws = jax.random.uniform(jax.random.fold_in(jax.random.fold_in(stream_key, 6), position), (shards_of,), jnp.float32, smallest / len(shards), high / len(shards))
        factor_of = factor_of * jnp.repeat(jnp.exp(draws), dims[position] // shards_of).reshape((-1,) + (1,) * (len(dims) - 1 - position))
    return factor_of


def bell_draw(key, extent, scale, most, cuts=(), kind=jnp.bfloat16):
    entries = jax.random.normal(key, extent, jnp.float32) * scale
    if len(cuts) > 0:
        entries = steps_of(key, extent, cuts, -0.22, 0.18) * entries
    return jnp.clip(entries, min=-most, max=most).astype(kind)


def setup_inputs(seed: int = 0) -> dict:
    arg_keys = jax.random.split(jax.random.key(seed), 18)
    tokens = bell_draw(arg_keys[0], (TOKENS, D), 1.0, 6.0, ((0, 32),))
    cotangent = bell_draw(arg_keys[1], (TOKENS, D), 1.0, 6.0, ((0, 32),))
    qkv_weight = bell_draw(arg_keys[2], (D, (HEADS + 2 * KV_HEADS) * HEAD_DIM), D ** -0.5, 0.1875, ((0, 8),), jnp.float32)
    out_weight = bell_draw(arg_keys[3], (D, D), (D // 32) ** -0.5, 1.0, ((0, 8),), jnp.float32)
    gateup_weight = bell_draw(arg_keys[4], (D, 2 * FF), D ** -0.5, 0.1875, ((0, 8),), jnp.float32)
    down_weight = bell_draw(arg_keys[5], (FF, D), FF ** -0.5, 0.09375, ((0, 8),), jnp.float32)
    norm_gains = jnp.clip(1.0 + 0.1 * jax.random.normal(arg_keys[6], (GAINS,), jnp.float32), 0.5, 1.5)
    avg_qkv = bell_draw(arg_keys[7], (D, (HEADS + 2 * KV_HEADS) * HEAD_DIM), (0.11 * (2.0 * TOKENS) ** 0.5), 160.0, ((0, 8),), jnp.float32)
    avg_out = bell_draw(arg_keys[8], (D, D), (0.11 * (0.02 * TOKENS) ** 0.5), 16.0, ((0, 8),), jnp.float32)
    avg_gateup = bell_draw(arg_keys[9], (D, 2 * FF), (0.11 * (0.3 * TOKENS) ** 0.5), 64.0, ((0, 8),), jnp.float32)
    avg_down = bell_draw(arg_keys[10], (FF, D), (0.11 * (0.3 * TOKENS) ** 0.5), 64.0, ((0, 8),), jnp.float32)
    avg_gains = bell_draw(arg_keys[11], (GAINS,), (0.11 * (4.0 * TOKENS) ** 0.5), 256.0, ((0, 8),), jnp.float32)
    sq_qkv = jnp.clip(jnp.exp(math.log(262.144) - 1.3862944 * jax.random.uniform(arg_keys[12], (D, (HEADS + 2 * KV_HEADS) * HEAD_DIM), jnp.float32) ** steps_of(arg_keys[12], (D, (HEADS + 2 * KV_HEADS) * HEAD_DIM), ((0, 8),), -0.2, 0.2)), 65.536, 262.144)
    sq_out = jnp.clip(jnp.exp(math.log(2.62144) - 1.3862944 * jax.random.uniform(arg_keys[13], (D, D), jnp.float32) ** steps_of(arg_keys[13], (D, D), ((0, 8),), -0.2, 0.2)), 0.65536, 2.62144)
    sq_gateup = jnp.clip(jnp.exp(math.log(39.3216) - 1.3862944 * jax.random.uniform(arg_keys[14], (D, 2 * FF), jnp.float32) ** steps_of(arg_keys[14], (D, 2 * FF), ((0, 8),), -0.2, 0.2)), 9.8304, 39.3216)
    sq_down = jnp.clip(jnp.exp(math.log(39.3216) - 1.3862944 * jax.random.uniform(arg_keys[15], (FF, D), jnp.float32) ** steps_of(arg_keys[15], (FF, D), ((0, 8),), -0.2, 0.2)), 9.8304, 39.3216)
    sq_gains = jnp.clip(jnp.exp(math.log(524.288) - 1.3862944 * jax.random.uniform(arg_keys[16], (GAINS,), jnp.float32) ** steps_of(arg_keys[16], (GAINS,), ((0, 8),), -0.2, 0.2)), 131.072, 524.288)
    return {"tokens": tokens, "cotangent": cotangent, "qkv_weight": qkv_weight, "out_weight": out_weight, "gateup_weight": gateup_weight, "down_weight": down_weight, "norm_gains": norm_gains, "avg_qkv": avg_qkv, "avg_out": avg_out, "avg_gateup": avg_gateup, "avg_down": avg_down, "avg_gains": avg_gains, "sq_qkv": sq_qkv, "sq_out": sq_out, "sq_gateup": sq_gateup, "sq_down": sq_down, "sq_gains": sq_gains}


NORM_EPS = 1e-05
THETA_BASE = 1000000.0
BETA_ONE = 0.9
BETA_TWO = 0.999
ADAM_EPS = 1e-08
RATE_QKV = 0.08
RATE_OUT = 0.4
RATE_GATEUP = 0.08
RATE_DOWN = 0.04
GAIN_RATE = 0.5
DECAY_RATE = 0.1
MASK_FILL = -1e+30

@jax.custom_vjp
def low(v):
    return lax.optimization_barrier(v.astype(jnp.bfloat16)).astype(jnp.float32)

@jax.custom_vjp
def low_back(v):
    return v

def low_keep(v):
    return (low(v), None)

def low_pass(kept, grad):
    return (grad,)

def back_keep(v):
    return (v, None)

def back_low(kept, grad):
    return (low(grad),)
low.defvjp(low_keep, low_pass)
low_back.defvjp(back_keep, back_low)

def matmul(left, right):
    return jnp.dot(left, right, precision=lax.Precision.HIGHEST, preferred_element_type=jnp.float32)

def rms_norm(values, gain):
    return values * lax.rsqrt(lax.optimization_barrier(jnp.mean(values * values, axis=-1, keepdims=True)) + NORM_EPS) * gain

def rotate(values, positions):
    half_dim = values.shape[-1] // 2
    frequency = THETA_BASE ** (-jnp.arange(half_dim, dtype=jnp.float32) * 2.0 / values.shape[-1])
    angles = positions.astype(jnp.float32)[:, None] * frequency[None, :]
    cosine = jnp.cos(angles)[:, None, :]
    sine_part = jnp.sin(angles)[:, None, :]
    lower_half = values[..., :half_dim]
    upper_half = values[..., half_dim:]
    return jnp.concatenate([lower_half * cosine - upper_half * sine_part, upper_half * cosine + lower_half * sine_part], axis=-1)

def attend(seq_item):
    query_heads, key_heads, value_heads = seq_item
    length = query_heads.shape[0]
    query_heads = query_heads.reshape(length, KV_HEADS, HEADS // KV_HEADS, HEAD_DIM)
    scores = jnp.einsum('qgrd,kgd->grqk', query_heads, key_heads, precision=lax.Precision.HIGHEST) * HEAD_DIM ** (-0.5)
    scores = low_back(scores)
    places = jnp.arange(length)
    allowed = places[None, :] <= places[:, None]
    scores = jnp.where(allowed, scores, MASK_FILL)
    row_max = lax.optimization_barrier(jnp.max(scores, axis=-1, keepdims=True))
    log_total = jnp.log(lax.optimization_barrier(jnp.sum(jnp.exp(scores - row_max), axis=-1, keepdims=True))) + row_max
    attn_probs = low(jnp.exp(scores - log_total))
    attended = jnp.einsum('grqk,kgd->qgrd', attn_probs, value_heads, precision=lax.Precision.HIGHEST)
    return attended.reshape(length, HEADS * HEAD_DIM)

def forward(parameters, inputs):
    qkv_full, out_full, gateup_full, down_full, gain_full = [low(item) for item in parameters]
    seq_count, length, width = inputs.shape
    flat = inputs.reshape(seq_count * length, width)
    norm_one = gain_full[:D]
    norm_two = gain_full[D:2 * D]
    query_gain = gain_full[2 * D:2 * D + HEAD_DIM]
    key_gain = gain_full[2 * D + HEAD_DIM:]
    query_width = HEADS * HEAD_DIM
    key_width = KV_HEADS * HEAD_DIM
    hidden_one = low(rms_norm(flat, norm_one))
    packed = low_back(matmul(hidden_one, qkv_full))
    query_heads = packed[:, :query_width].reshape(seq_count, length, HEADS, HEAD_DIM)
    key_heads = packed[:, query_width:query_width + key_width].reshape(seq_count, length, KV_HEADS, HEAD_DIM)
    value_heads = packed[:, query_width + key_width:].reshape(seq_count, length, KV_HEADS, HEAD_DIM)
    positions = jnp.arange(length)
    query_heads = low(rotate(rms_norm(query_heads, query_gain), positions))
    key_heads = low(rotate(rms_norm(key_heads, key_gain), positions))
    value_heads = low(value_heads)
    attended = lax.map(jax.checkpoint(attend), (query_heads, key_heads, value_heads))
    attended = low(low_back(attended)).reshape(seq_count * length, query_width)
    branch = low_back(matmul(attended, out_full))
    middle = flat + branch
    hidden_two = low(rms_norm(middle, norm_two))
    gateup = low_back(matmul(hidden_two, gateup_full))
    activated = low(jax.nn.silu(gateup[:, :FF]) * gateup[:, FF:])
    result = middle + matmul(activated, down_full)
    return result.reshape(seq_count, length, width)

def adam_step(weight_now, grad_now, moment_one, moment_two, rate, decay):
    moment_one = BETA_ONE * moment_one + (1.0 - BETA_ONE) * grad_now
    moment_two = BETA_TWO * moment_two + (1.0 - BETA_TWO) * grad_now * grad_now
    corrected_one = moment_one / (1.0 - BETA_ONE ** STEP)
    corrected_two = moment_two / (1.0 - BETA_TWO ** STEP)
    weight_new = weight_now - rate * (corrected_one / (jnp.sqrt(corrected_two) + ADAM_EPS) + decay * weight_now)
    return (weight_new, moment_one, moment_two)

def reference(tokens, cotangent, qkv_weight, out_weight, gateup_weight, down_weight, norm_gains, avg_qkv, avg_out, avg_gateup, avg_down, avg_gains, sq_qkv, sq_out, sq_gateup, sq_down, sq_gains):
    parameters = (qkv_weight, out_weight, gateup_weight, down_weight, norm_gains)
    inputs = tokens.astype(jnp.float32).reshape(-1, 4, LEN, D)
    backs = cotangent.astype(jnp.float32).reshape(-1, 4, LEN, D)

    def accumulate(running, seq_item):
        block_in, block_back = seq_item
        result, pullback = jax.vjp(forward, parameters, block_in)
        gradients, grad_in = pullback(block_back)
        running = tuple((old + new for old, new in zip(running, gradients)))
        return (running, (result.astype(jnp.bfloat16), grad_in.astype(jnp.bfloat16)))
    zero_sums = tuple((jnp.zeros(item.shape, jnp.float32) for item in parameters))
    gradients, (outputs, grad_inputs) = lax.scan(accumulate, zero_sums, (inputs, backs))
    firsts = (avg_qkv, avg_out, avg_gateup, avg_down, avg_gains)
    seconds = (sq_qkv, sq_out, sq_gateup, sq_down, sq_gains)
    rates = (RATE_QKV, RATE_OUT, RATE_GATEUP, RATE_DOWN, GAIN_RATE)
    decays = (DECAY_RATE, DECAY_RATE, DECAY_RATE, DECAY_RATE, 0.0)
    new_weights = []
    new_firsts = []
    new_seconds = []
    for index_one in range(5):
        weight_new, moment_one, moment_two = adam_step(parameters[index_one], gradients[index_one], firsts[index_one], seconds[index_one], rates[index_one], decays[index_one])
        new_weights.append(weight_new)
        new_firsts.append(moment_one)
        new_seconds.append(moment_two)
    return (outputs.reshape(-1, D), grad_inputs.reshape(-1, D), gradients[0], gradients[1], gradients[2], gradients[3], gradients[4], new_weights[0], new_weights[1], new_weights[2], new_weights[3], new_weights[4], new_firsts[0], new_firsts[1], new_firsts[2], new_firsts[3], new_firsts[4], new_seconds[0], new_seconds[1], new_seconds[2], new_seconds[3], new_seconds[4])
```

```python
from functools import partial

import jax
import jax.numpy as jnp
from jax import lax
from jax.experimental import pallas as pl
from jax.experimental.pallas import tpu as pltpu
from jax.sharding import PartitionSpec as P

D = 1024
HEADS = 16
KV_HEADS = 8
HEAD_DIM = 64
FF = 4608
LEN = 1024
STEP = 10


NORM_EPS = 1e-05
THETA_BASE = 1000000.0
BETA_ONE = 0.9
BETA_TWO = 0.999
ADAM_EPS = 1e-08
RATE_QKV = 0.08
RATE_OUT = 0.4
RATE_GATEUP = 0.08
RATE_DOWN = 0.04
GAIN_RATE = 0.5
DECAY_RATE = 0.1
MASK_FILL = -1e30


MESH = pl.DeviceIdType.MESH
GAIN_ROWS = 8

ORDER_A = ("top", "mid", "low", "x", "core")
ORDER_B = ("top", "x", "mid", "low", "core")
ORDER_C = ("top", "low", "x", "mid", "core")
CHUNKS = (
    (0, 0, 2, ORDER_B),
    (0, 1, 2, ORDER_C),
    (1, 0, 1, ORDER_A),
    (2, 0, 3, ORDER_A),
    (2, 1, 3, ORDER_B),
    (2, 2, 3, ORDER_C),
    (3, 0, 2, ORDER_A),
    (3, 1, 2, ORDER_B),
)


def gather_kernel(tops, *refs):
    pieces, gain_in = refs[0:4], refs[4]
    fulls, gain_out = refs[5:9], refs[9]
    send_sem, recv_sem, gain_send, gain_recv, local_sem = refs[10:]
    rep = lax.axis_index("rep")
    shard = lax.axis_index("shard")
    x, core = rep // 2, rep % 2
    top, mid, low = shard // 4, (shard // 2) % 2, shard % 2
    quarter = core * 2 + x

    partners = {
        "top": [(rep, ((top + j) % tops) * 4 + mid * 2 + low) for j in range(1, tops)],
        "mid": [(rep, top * 4 + (1 - mid) * 2 + low)],
        "low": [(rep, top * 4 + mid * 2 + (1 - low))],
        "x": [((1 - x) * 2 + core, shard)],
        "core": [(x * 2 + (1 - core), shard)],
    }
    everyone = [peer for name in ORDER_A for peer in partners[name]]
    barrier = pltpu.get_barrier_semaphore()
    for peer in everyone:
        pl.semaphore_signal(barrier, inc=1, device_id=peer, device_id_type=MESH)

    own = []
    for index in range(4):
        width = pieces[index].shape[1]
        place = fulls[index].at[
            top, mid, low, :, pl.ds(pl.multiple_of(quarter * width, 128), width)
        ]
        own.append(pltpu.make_async_copy(pieces[index], place, local_sem.at[index]))
    own.append(pltpu.make_async_copy(gain_in, gain_out.at[top, mid, low], local_sem.at[4]))
    for copy in own:
        copy.start()
    for copy in own:
        copy.wait()
    pl.semaphore_wait(barrier, len(everyone))

    def region(chunk, done):
        matrix, part, parts, _ = chunk
        full = fulls[matrix]
        width = full.shape[-1] // 4
        step = width // parts
        rows = [
            pl.ds(0, size) if name in done else pl.ds(value, 1)
            for name, value, size in (("top", top, tops), ("mid", mid, 2), ("low", low, 2))
        ]
        starts = []
        for c in (0, 1) if "core" in done else (core,):
            for xx in (0, 1) if "x" in done else (x,):
                starts.append((c * 2 + xx) * width + part * step)
        return [
            full.at[
                rows[0],
                rows[1],
                rows[2],
                :,
                pl.ds(pl.multiple_of(start, 128), step),
            ]
            for start in starts
        ]

    started = []

    def start_step(index, step):
        order = CHUNKS[index][3]
        views = region(CHUNKS[index], order[:step])
        copies = []
        slot = 0
        for peer in partners[order[step]]:
            for view in views:
                copies.append(
                    pltpu.make_async_remote_copy(
                        src_ref=view,
                        dst_ref=view,
                        send_sem=send_sem.at[index, step, slot],
                        recv_sem=recv_sem.at[index, step, slot],
                        device_id=peer,
                        device_id_type=MESH,
                    )
                )
                slot += 1
        for copy in copies:
            copy.start()
        started.extend(copies)
        return copies

    def start_gain(step):
        name = ("top", "mid", "low")[step]
        rows = [
            pl.ds(0, size) if step > place else pl.ds(value, 1)
            for place, (value, size) in enumerate(((top, tops), (mid, 2), (low, 2)))
        ]
        view = gain_out.at[rows[0], rows[1], rows[2]]
        copies = []
        for slot, peer in enumerate(partners[name]):
            copies.append(
                pltpu.make_async_remote_copy(
                    src_ref=view,
                    dst_ref=view,
                    send_sem=gain_send.at[step, slot],
                    recv_sem=gain_recv.at[step, slot],
                    device_id=peer,
                    device_id_type=MESH,
                )
            )
        for copy in copies:
            copy.start()
        started.extend(copies)
        return copies

    gain_flight = start_gain(0)
    flight = [start_step(index, 0) for index in range(len(CHUNKS))]
    for step in range(1, 6):
        for index in range(len(CHUNKS)):
            for copy in flight[index]:
                copy.wait_recv()
            if step < 5:
                flight[index] = start_step(index, step)
        if step < 4:
            for copy in gain_flight:
                copy.wait_recv()
            if step < 3:
                gain_flight = start_gain(step)
    for copy in started:
        copy.wait_send()


def gather_weights(masters):
    matrices, gains = masters[:4], masters[4]
    shards = lax.axis_size("shard")
    tops = shards // 4
    rep = lax.axis_index("rep")
    quarter = (rep % 2) * 2 + rep // 2
    pieces = []
    for item in matrices:
        width = item.shape[1] // 4
        pieces.append(
            lax.dynamic_slice_in_dim(item, quarter * width, width, axis=1).astype(jnp.bfloat16)
        )
    count = gains.shape[0]
    gain_piece = jnp.pad(gains, (0, GAIN_ROWS * 128 - count)).reshape(GAIN_ROWS, 128)
    slots = max(2, tops - 1)
    outs = [
        jax.ShapeDtypeStruct((tops, 2, 2) + item.shape, jnp.bfloat16) for item in matrices
    ] + [jax.ShapeDtypeStruct((tops, 2, 2, GAIN_ROWS, 128), jnp.float32)]
    results = pl.pallas_call(
        partial(gather_kernel, tops),
        out_shape=outs,
        in_specs=[pl.BlockSpec(memory_space=pl.ANY)] * 5,
        out_specs=[pl.BlockSpec(memory_space=pl.ANY)] * 5,
        scratch_shapes=[
            pltpu.SemaphoreType.DMA((len(CHUNKS), 5, slots)),
            pltpu.SemaphoreType.DMA((len(CHUNKS), 5, slots)),
            pltpu.SemaphoreType.DMA((3, slots)),
            pltpu.SemaphoreType.DMA((3, slots)),
            pltpu.SemaphoreType.DMA((5,)),
        ],
        compiler_params=pltpu.CompilerParams(collective_id=0, has_side_effects=True),
        name="gather_weights",
    )(*pieces, gain_piece)
    fulls = [
        full.reshape(shards * item.shape[0], item.shape[1])
        for full, item in zip(results[:4], matrices)
    ]
    gain_full = (
        results[4].reshape(shards, GAIN_ROWS * 128)[:, :count].reshape(-1).astype(jnp.bfloat16)
    )
    return (*fulls, gain_full)


def swap(part, axis_name, digit):
    size = lax.axis_size(axis_name)
    return lax.ppermute(part, axis_name, [(i, i ^ digit) for i in range(size)])


def reduce_chunk(total, turn):
    shards = lax.axis_size("shard")
    digits = shards.bit_length() - 1
    rep = lax.axis_index("rep")
    shard = lax.axis_index("shard")
    rows, columns = total.shape
    total = total.reshape((2,) * digits + (rows // shards, columns))
    left = list(range(digits))[::-1]
    first = ["x", 0, 1]
    first = first[turn:] + first[:turn]
    for name in ["core"] + first + left[:-2]:
        if name in ("core", "x"):
            digit = 1 if name == "core" else 2
            mine = (rep // digit) % 2
            axis = total.ndim - 1
            half = total.shape[axis] // 2
            send = lax.dynamic_slice_in_dim(total, (1 - mine) * half, half, axis=axis)
            keep = lax.dynamic_slice_in_dim(total, mine * half, half, axis=axis)
            got = swap(send, "rep", digit)
        else:
            mine = (shard // 2**name) % 2
            axis = left.index(name)
            left.remove(name)
            send = lax.dynamic_index_in_dim(total, 1 - mine, axis, keepdims=False)
            keep = lax.dynamic_index_in_dim(total, mine, axis, keepdims=False)
            got = swap(send, "shard", 2**name)
        total = (keep.astype(jnp.float32) + got.astype(jnp.float32)).astype(jnp.bfloat16)
    return total


def reduce_matrix(chunks, turns):
    parts = [reduce_chunk(chunk, turn) for chunk, turn in zip(chunks, turns)]
    piece = jnp.stack(parts, axis=1)
    rows, count, width = piece.shape
    every = lax.all_gather(piece, "rep", axis=0, tiled=False)
    every = every.reshape(2, 2, rows, count, width).transpose(2, 3, 1, 0, 4)
    return every.reshape(rows, count * 4 * width).astype(jnp.float32)


def rms_norm(values, gain):
    return values * lax.rsqrt(jnp.mean(values * values, axis=-1, keepdims=True) + NORM_EPS) * gain


def rotate(values, positions):
    half_dim = values.shape[-1] // 2
    frequency = THETA_BASE ** (-jnp.arange(half_dim, dtype=jnp.float32) * 2.0 / values.shape[-1])
    angles = positions.astype(jnp.float32)[:, None] * frequency[None, :]
    cosine = jnp.cos(angles)[:, None, :]
    sine_part = jnp.sin(angles)[:, None, :]
    lower_half = values[..., :half_dim]
    upper_half = values[..., half_dim:]
    return jnp.concatenate(
        [
            lower_half * cosine - upper_half * sine_part,
            upper_half * cosine + lower_half * sine_part,
        ],
        axis=-1,
    )


def head_inputs(qk_raw, query_gain, key_gain, positions):
    row_count = qk_raw.shape[0]
    query_width = HEADS * HEAD_DIM
    query_heads = qk_raw[:, :query_width].reshape(row_count, HEADS, HEAD_DIM)
    key_heads = qk_raw[:, query_width:].reshape(row_count, KV_HEADS, HEAD_DIM)
    return (
        rotate(rms_norm(query_heads, query_gain), positions),
        rotate(rms_norm(key_heads, key_gain), positions),
    )


def swiglu(gateup):
    return jax.nn.silu(gateup[:, :FF]) * gateup[:, FF:]


def masked_scores(query_heads, key_heads, start_row):
    scores = jnp.einsum(
        "qgrd,kgd->grqk", query_heads, key_heads, preferred_element_type=jnp.float32
    ) * HEAD_DIM ** (-0.5)
    query_places = start_row + jnp.arange(query_heads.shape[0])
    allowed = jnp.arange(key_heads.shape[0])[None, :] <= query_places[:, None]
    return jnp.where(allowed, scores, MASK_FILL)


def forward_seq(seq_item):
    query_heads, key_heads, value_heads = seq_item
    length = query_heads.shape[0]
    block_rows = min(512, length)
    outputs = []
    log_parts = []
    for start_row in range(0, length, block_rows):
        stop_row = start_row + block_rows
        scores = masked_scores(query_heads[start_row:stop_row], key_heads[:stop_row], start_row)
        row_max = jnp.max(scores, axis=-1, keepdims=True)
        log_total = jnp.log(jnp.sum(jnp.exp(scores - row_max), axis=-1, keepdims=True)) + row_max
        attn_probs = jnp.exp(scores - log_total).astype(jnp.bfloat16)
        outputs.append(
            jnp.einsum(
                "grqk,kgd->qgrd",
                attn_probs,
                value_heads[:stop_row],
                preferred_element_type=jnp.float32,
            )
        )
        log_parts.append(log_total)
    return (jnp.concatenate(outputs, axis=0), jnp.concatenate(log_parts, axis=2))


def backward_seq(seq_item):
    query_heads, key_heads, value_heads, log_totals, grad_att = seq_item
    length = query_heads.shape[0]
    block_rows = min(512, length)
    score_scale = HEAD_DIM ** (-0.5)
    grad_keys = jnp.zeros(key_heads.shape, jnp.float32)
    grad_values = jnp.zeros(value_heads.shape, jnp.float32)
    query_parts = []
    for start_row in range(0, length, block_rows):
        stop_row = start_row + block_rows
        scores = masked_scores(query_heads[start_row:stop_row], key_heads[:stop_row], start_row)
        attn_probs = jnp.exp(scores - log_totals[:, :, start_row:stop_row])
        grad_probs = jnp.einsum(
            "qgrd,kgd->grqk",
            grad_att[start_row:stop_row],
            value_heads[:stop_row],
            preferred_element_type=jnp.float32,
        )
        grad_values = grad_values.at[:stop_row].add(
            jnp.einsum(
                "grqk,qgrd->kgd",
                attn_probs.astype(jnp.bfloat16),
                grad_att[start_row:stop_row],
                preferred_element_type=jnp.float32,
            )
        )
        row_inner = jnp.sum(attn_probs * grad_probs, axis=-1, keepdims=True)
        grad_scores = (attn_probs * (grad_probs - row_inner)).astype(jnp.bfloat16)
        query_parts.append(
            jnp.einsum(
                "grqk,kgd->qgrd",
                grad_scores,
                key_heads[:stop_row],
                preferred_element_type=jnp.float32,
            )
            * score_scale
        )
        grad_keys = grad_keys.at[:stop_row].add(
            jnp.einsum(
                "grqk,qgrd->kgd",
                grad_scores,
                query_heads[start_row:stop_row],
                preferred_element_type=jnp.float32,
            )
            * score_scale
        )
    return (jnp.concatenate(query_parts, axis=0), grad_keys, grad_values)


def adam_step(weight_now, grad_now, moment_one, moment_two, rate, decay):
    moment_one = BETA_ONE * moment_one + (1.0 - BETA_ONE) * grad_now
    moment_two = BETA_TWO * moment_two + (1.0 - BETA_TWO) * grad_now * grad_now
    corrected_one = moment_one / (1.0 - BETA_ONE**STEP)
    corrected_two = moment_two / (1.0 - BETA_TWO**STEP)
    weight_new = weight_now - rate * (
        corrected_one / (jnp.sqrt(corrected_two) + ADAM_EPS) + decay * weight_now
    )
    return (weight_new, moment_one, moment_two)


def local(
    tokens,
    cotangent,
    qkv_weight,
    out_weight,
    gateup_weight,
    down_weight,
    norm_gains,
    avg_qkv,
    avg_out,
    avg_gateup,
    avg_down,
    avg_gains,
    sq_qkv,
    sq_out,
    sq_gateup,
    sq_down,
    sq_gains,
):
    masters = (qkv_weight, out_weight, gateup_weight, down_weight, norm_gains)
    weights = gather_weights(masters)
    qkv_full, out_full, gateup_full, down_full, gain_full = weights
    gain_values = gain_full.astype(jnp.float32)
    norm_one = gain_values[:D]
    norm_two = gain_values[D : 2 * D]
    query_gain = gain_values[2 * D : 2 * D + HEAD_DIM]
    key_gain = gain_values[2 * D + HEAD_DIM :]
    row_count = tokens.shape[0]
    seq_count = row_count // LEN
    group_ratio = HEADS // KV_HEADS
    query_width = HEADS * HEAD_DIM
    key_width = KV_HEADS * HEAD_DIM
    positions = jnp.arange(row_count) % LEN
    inputs = tokens.astype(jnp.float32)
    hidden_one = rms_norm(inputs, norm_one).astype(jnp.bfloat16)
    packed = jnp.dot(hidden_one, qkv_full, preferred_element_type=jnp.float32)
    qk_raw = packed[:, : query_width + key_width]
    head_fn = partial(head_inputs, positions=positions)
    rotated_query, rotated_keys = head_fn(qk_raw, query_gain, key_gain)
    query_heads = rotated_query.astype(jnp.bfloat16).reshape(
        seq_count, LEN, KV_HEADS, group_ratio, HEAD_DIM
    )
    key_heads = rotated_keys.astype(jnp.bfloat16).reshape(seq_count, LEN, KV_HEADS, HEAD_DIM)
    value_heads = (
        packed[:, query_width + key_width :]
        .astype(jnp.bfloat16)
        .reshape(seq_count, LEN, KV_HEADS, HEAD_DIM)
    )
    attended, log_totals = lax.map(forward_seq, (query_heads, key_heads, value_heads))
    attended = attended.reshape(row_count, query_width).astype(jnp.bfloat16)
    branch = jnp.dot(attended, out_full, preferred_element_type=jnp.float32)
    middle = inputs + branch
    hidden_two = rms_norm(middle, norm_two).astype(jnp.bfloat16)
    gateup = jnp.dot(hidden_two, gateup_full, preferred_element_type=jnp.float32)
    activated = swiglu(gateup).astype(jnp.bfloat16)
    result = middle + jnp.dot(activated, down_full, preferred_element_type=jnp.float32)
    block_out = result.astype(jnp.bfloat16)
    qkv_back, out_back, gateup_back, down_back = weights[:4]
    grad_down = jnp.einsum("tf,td->fd", activated, cotangent, preferred_element_type=jnp.float32)
    grad_down = grad_down.astype(jnp.bfloat16)
    grad_act = jnp.einsum("td,fd->tf", cotangent, down_back, preferred_element_type=jnp.float32)
    unused_act, pullback = jax.vjp(swiglu, gateup)
    grad_gateup_raw = pullback(grad_act)[0].astype(jnp.bfloat16)
    grad_gateup = jnp.einsum(
        "td,tf->df", hidden_two, grad_gateup_raw, preferred_element_type=jnp.float32
    )
    grad_hidden2 = jnp.einsum(
        "tf,df->td", grad_gateup_raw, gateup_back, preferred_element_type=jnp.float32
    )
    grad_gateup = grad_gateup.astype(jnp.bfloat16)
    grad_hidden2, grad_down, grad_gateup = lax.optimization_barrier(
        (grad_hidden2, grad_down, grad_gateup)
    )
    summed_gateup = reduce_matrix(jnp.split(grad_gateup, 3, axis=1), (0, 1, 2))
    summed_down = reduce_matrix(jnp.split(grad_down, 2, axis=1), (0, 1))
    unused_two, pullback = jax.vjp(rms_norm, middle, norm_two)
    grad_midpart, grad_norm2 = pullback(grad_hidden2)
    grad_middle = cotangent.astype(jnp.float32) + grad_midpart
    grad_branch = grad_middle.astype(jnp.bfloat16)
    grad_out = jnp.einsum("tq,td->qd", attended, grad_branch, preferred_element_type=jnp.float32)
    summed_out = reduce_matrix([grad_out.astype(jnp.bfloat16)], (2,))
    grad_att = jnp.einsum(
        "td,qd->tq", grad_branch, out_back, preferred_element_type=jnp.float32
    ).astype(jnp.bfloat16)
    grad_att = grad_att.reshape(seq_count, LEN, KV_HEADS, group_ratio, HEAD_DIM)
    grad_query, grad_keys, grad_values = lax.map(
        backward_seq, (query_heads, key_heads, value_heads, log_totals, grad_att)
    )
    unused_heads, pullback = jax.vjp(head_fn, qk_raw, query_gain, key_gain)
    grad_qkraw, grad_qgain, grad_kgain = pullback(
        (
            grad_query.reshape(row_count, HEADS, HEAD_DIM),
            grad_keys.reshape(row_count, KV_HEADS, HEAD_DIM),
        )
    )
    grad_packed = jnp.concatenate(
        [grad_qkraw, grad_values.reshape(row_count, key_width)], axis=1
    ).astype(jnp.bfloat16)
    grad_qkv = jnp.einsum("td,tp->dp", hidden_one, grad_packed, preferred_element_type=jnp.float32)
    grad_hidden1 = jnp.einsum(
        "tp,dp->td", grad_packed, qkv_back, preferred_element_type=jnp.float32
    )
    unused_one, pullback = jax.vjp(rms_norm, inputs, norm_one)
    grad_inpart, grad_norm1 = pullback(grad_hidden1)
    grad_tokens = (grad_middle + grad_inpart).astype(jnp.bfloat16)
    grad_gains = jnp.concatenate([grad_norm1, grad_norm2, grad_qgain, grad_kgain], axis=0)
    summed_qkv = reduce_matrix(jnp.split(grad_qkv.astype(jnp.bfloat16), 2, axis=1), (1, 2))
    gain_rows = norm_gains.shape[0]
    all_gains = lax.psum(grad_gains, ("rep", "shard"))
    summed_gains = lax.dynamic_slice_in_dim(
        all_gains, lax.axis_index("shard") * gain_rows, gain_rows, axis=0
    )
    summed = (summed_qkv, summed_out, summed_gateup, summed_down, summed_gains)
    firsts = (avg_qkv, avg_out, avg_gateup, avg_down, avg_gains)
    seconds = (sq_qkv, sq_out, sq_gateup, sq_down, sq_gains)
    rates = (RATE_QKV, RATE_OUT, RATE_GATEUP, RATE_DOWN, GAIN_RATE)
    decays = (DECAY_RATE, DECAY_RATE, DECAY_RATE, DECAY_RATE, 0.0)
    new_weights = []
    new_firsts = []
    new_seconds = []
    for index_one in range(5):
        weight_new, moment_one, moment_two = adam_step(
            masters[index_one],
            summed[index_one],
            firsts[index_one],
            seconds[index_one],
            rates[index_one],
            decays[index_one],
        )
        new_weights.append(weight_new)
        new_firsts.append(moment_one)
        new_seconds.append(moment_two)
    return (
        (block_out, grad_tokens)
        + summed
        + tuple(new_weights)
        + tuple(new_firsts)
        + tuple(new_seconds)
    )


def solution(mesh):
    in_specs = (
        P(("rep", "shard"), None),
        P(("rep", "shard"), None),
        P("shard", None),
        P("shard", None),
        P("shard", None),
        P("shard", None),
        P("shard"),
        P("shard", None),
        P("shard", None),
        P("shard", None),
        P("shard", None),
        P("shard"),
        P("shard", None),
        P("shard", None),
        P("shard", None),
        P("shard", None),
        P("shard"),
    )
    out_specs = (
        P(("rep", "shard"), None),
        P(("rep", "shard"), None),
        P("shard", None),
        P("shard", None),
        P("shard", None),
        P("shard", None),
        P("shard"),
        P("shard", None),
        P("shard", None),
        P("shard", None),
        P("shard", None),
        P("shard"),
        P("shard", None),
        P("shard", None),
        P("shard", None),
        P("shard", None),
        P("shard"),
        P("shard", None),
        P("shard", None),
        P("shard", None),
        P("shard", None),
        P("shard"),
    )
    return jax.shard_map(local, mesh=mesh, in_specs=in_specs, out_specs=out_specs, check_vma=False)
```

```python
from functools import partial

import jax
import jax.numpy as jnp
from jax import lax
from jax.experimental import pallas as pl
from jax.experimental.pallas import tpu as pltpu
from jax.sharding import PartitionSpec as P

D = 1024
HEADS = 16
KV_HEADS = 8
HEAD_DIM = 64
FF = 4608
LEN = 1024
STEP = 10


NORM_EPS = 1e-05
THETA_BASE = 1000000.0
BETA_ONE = 0.9
BETA_TWO = 0.999
ADAM_EPS = 1e-08
RATE_QKV = 0.08
RATE_OUT = 0.4
RATE_GATEUP = 0.08
RATE_DOWN = 0.04
GAIN_RATE = 0.5
DECAY_RATE = 0.1
MASK_FILL = -1e30


MESH = pl.DeviceIdType.MESH
GAIN_ROWS = 8

ORDER_A = ("top", "mid", "low", "x", "core")
ORDER_B = ("top", "x", "mid", "low", "core")
ORDER_C = ("top", "low", "x", "mid", "core")
CHUNKS = (
    (0, 0, 2, ORDER_B),
    (0, 1, 2, ORDER_C),
    (1, 0, 1, ORDER_A),
    (2, 0, 3, ORDER_A),
    (2, 1, 3, ORDER_B),
    (2, 2, 3, ORDER_C),
    (3, 0, 2, ORDER_A),
    (3, 1, 2, ORDER_B),
)


def gather_kernel(tops, *refs):
    pieces, gain_in = refs[0:4], refs[4]
    fulls, gain_out = refs[5:9], refs[9]
    send_sem, recv_sem, gain_send, gain_recv, local_sem = refs[10:]
    rep = lax.axis_index("rep")
    shard = lax.axis_index("shard")
    x, core = rep // 2, rep % 2
    top, mid, low = shard // 4, (shard // 2) % 2, shard % 2
    quarter = core * 2 + x

    partners = {
        "top": [(rep, ((top + j) % tops) * 4 + mid * 2 + low) for j in range(1, tops)],
        "mid": [(rep, top * 4 + (1 - mid) * 2 + low)],
        "low": [(rep, top * 4 + mid * 2 + (1 - low))],
        "x": [((1 - x) * 2 + core, shard)],
        "core": [(x * 2 + (1 - core), shard)],
    }
    everyone = [peer for name in ORDER_A for peer in partners[name]]
    barrier = pltpu.get_barrier_semaphore()
    for peer in everyone:
        pl.semaphore_signal(barrier, inc=1, device_id=peer, device_id_type=MESH)

    own = []
    for index in range(4):
        width = pieces[index].shape[1]
        place = fulls[index].at[
            top, mid, low, :, pl.ds(pl.multiple_of(quarter * width, 128), width)
        ]
        own.append(pltpu.make_async_copy(pieces[index], place, local_sem.at[index]))
    own.append(pltpu.make_async_copy(gain_in, gain_out.at[top, mid, low], local_sem.at[4]))
    for copy in own:
        copy.start()
    for copy in own:
        copy.wait()
    pl.semaphore_wait(barrier, len(everyone))

    def region(chunk, done):
        matrix, part, parts, _ = chunk
        full = fulls[matrix]
        width = full.shape[-1] // 4
        step = width // parts
        rows = [
            pl.ds(0, size) if name in done else pl.ds(value, 1)
            for name, value, size in (("top", top, tops), ("mid", mid, 2), ("low", low, 2))
        ]
        starts = []
        for c in (0, 1) if "core" in done else (core,):
            for xx in (0, 1) if "x" in done else (x,):
                starts.append((c * 2 + xx) * width + part * step)
        return [
            full.at[
                rows[0],
                rows[1],
                rows[2],
                :,
                pl.ds(pl.multiple_of(start, 128), step),
            ]
            for start in starts
        ]

    started = []

    def start_step(index, step):
        order = CHUNKS[index][3]
        views = region(CHUNKS[index], order[:step])
        copies = []
        slot = 0
        for peer in partners[order[step]]:
            for view in views:
                copies.append(
                    pltpu.make_async_remote_copy(
                        src_ref=view,
                        dst_ref=view,
                        send_sem=send_sem.at[index, step, slot],
                        recv_sem=recv_sem.at[index, step, slot],
                        device_id=peer,
                        device_id_type=MESH,
                    )
                )
                slot += 1
        for copy in copies:
            copy.start()
        started.extend(copies)
        return copies

    def start_gain(step):
        name = ("top", "mid", "low")[step]
        rows = [
            pl.ds(0, size) if step > place else pl.ds(value, 1)
            for place, (value, size) in enumerate(((top, tops), (mid, 2), (low, 2)))
        ]
        view = gain_out.at[rows[0], rows[1], rows[2]]
        copies = []
        for slot, peer in enumerate(partners[name]):
            copies.append(
                pltpu.make_async_remote_copy(
                    src_ref=view,
                    dst_ref=view,
                    send_sem=gain_send.at[step, slot],
                    recv_sem=gain_recv.at[step, slot],
                    device_id=peer,
                    device_id_type=MESH,
                )
            )
        for copy in copies:
            copy.start()
        started.extend(copies)
        return copies

    gain_flight = start_gain(0)
    flight = [start_step(index, 0) for index in range(len(CHUNKS))]
    for step in range(1, 6):
        for index in range(len(CHUNKS)):
            for copy in flight[index]:
                copy.wait_recv()
            if step < 5:
                flight[index] = start_step(index, step)
        if step < 4:
            for copy in gain_flight:
                copy.wait_recv()
            if step < 3:
                gain_flight = start_gain(step)
    for copy in started:
        copy.wait_send()


def gather_weights(masters):
    matrices, gains = masters[:4], masters[4]
    shards = lax.axis_size("shard")
    tops = shards // 4
    rep = lax.axis_index("rep")
    quarter = (rep % 2) * 2 + rep // 2
    pieces = []
    for item in matrices:
        width = item.shape[1] // 4
        pieces.append(
            lax.dynamic_slice_in_dim(item, quarter * width, width, axis=1).astype(jnp.bfloat16)
        )
    count = gains.shape[0]
    gain_piece = jnp.pad(gains, (0, GAIN_ROWS * 128 - count)).reshape(GAIN_ROWS, 128)
    slots = max(2, tops - 1)
    outs = [
        jax.ShapeDtypeStruct((tops, 2, 2) + item.shape, jnp.bfloat16) for item in matrices
    ] + [jax.ShapeDtypeStruct((tops, 2, 2, GAIN_ROWS, 128), jnp.float32)]
    results = pl.pallas_call(
        partial(gather_kernel, tops),
        out_shape=outs,
        in_specs=[pl.BlockSpec(memory_space=pl.ANY)] * 5,
        out_specs=[pl.BlockSpec(memory_space=pl.ANY)] * 5,
        scratch_shapes=[
            pltpu.SemaphoreType.DMA((len(CHUNKS), 5, slots)),
            pltpu.SemaphoreType.DMA((len(CHUNKS), 5, slots)),
            pltpu.SemaphoreType.DMA((3, slots)),
            pltpu.SemaphoreType.DMA((3, slots)),
            pltpu.SemaphoreType.DMA((5,)),
        ],
        compiler_params=pltpu.CompilerParams(collective_id=0, has_side_effects=True),
        name="gather_weights",
    )(*pieces, gain_piece)
    fulls = [
        full.reshape(shards * item.shape[0], item.shape[1])
        for full, item in zip(results[:4], matrices)
    ]
    gain_full = (
        results[4].reshape(shards, GAIN_ROWS * 128)[:, :count].reshape(-1).astype(jnp.bfloat16)
    )
    return (*fulls, gain_full)


def swap(part, axis_name, digit):
    size = lax.axis_size(axis_name)
    return lax.ppermute(part, axis_name, [(i, i ^ digit) for i in range(size)])


def split_rows(chunks):
    shards = lax.axis_size("shard")
    digits = shards.bit_length() - 1
    return [
        chunk.reshape((2,) * digits + (chunk.shape[0] // shards, chunk.shape[1]))
        for chunk in chunks
    ]


def one_exchange(total, turn, step):
    digits = lax.axis_size("shard").bit_length() - 1
    left = list(range(digits))[::-1]
    first = ["x", 0, 1]
    first = first[turn:] + first[:turn]
    order = ["core"] + first + left[:-2]
    name = order[step]
    if name in ("core", "x"):
        digit = 1 if name == "core" else 2
        mine = (lax.axis_index("rep") // digit) % 2
        axis = total.ndim - 1
        half = total.shape[axis] // 2
        send = lax.dynamic_slice_in_dim(total, (1 - mine) * half, half, axis=axis)
        keep = lax.dynamic_slice_in_dim(total, mine * half, half, axis=axis)
        got = swap(send, "rep", digit)
    else:
        mine = (lax.axis_index("shard") // 2**name) % 2
        axis = [place for place in left if place not in order[:step]].index(name)
        send = lax.dynamic_index_in_dim(total, 1 - mine, axis, keepdims=False)
        keep = lax.dynamic_index_in_dim(total, mine, axis, keepdims=False)
        got = swap(send, "shard", 2**name)
    return (keep.astype(jnp.float32) + got.astype(jnp.float32)).astype(jnp.bfloat16)


class Staged:
    def __init__(self, chunks, turns):
        self.chunks = list(chunks)
        self.turns = turns
        self.taken = 0

    def advance(self, *values):
        count = len(self.chunks)
        totals = [
            one_exchange(chunk, turn, self.taken) for chunk, turn in zip(self.chunks, self.turns)
        ]
        self.taken += 1
        tied = lax.optimization_barrier((*totals, *values))
        self.chunks = list(tied[:count])
        out = tied[count:]
        return out if len(out) > 1 else out[0]

    def finish(self):
        shards = lax.axis_size("shard")
        steps = 2 + shards.bit_length() - 1
        while self.taken < steps:
            self.chunks = [
                one_exchange(chunk, turn, self.taken)
                for chunk, turn in zip(self.chunks, self.turns)
            ]
            self.taken += 1
        return self.chunks


def reduce_matrix(chunks, turns):
    staged = Staged(split_rows(chunks), turns)
    return gather_parts(staged.finish())


def gather_parts(parts):
    piece = jnp.stack(parts, axis=1)
    rows, count, width = piece.shape
    every = lax.all_gather(piece, "rep", axis=0, tiled=False)
    every = every.reshape(2, 2, rows, count, width).transpose(2, 3, 1, 0, 4)
    return every.reshape(rows, count * 4 * width).astype(jnp.float32)


def rms_norm(values, gain):
    return values * lax.rsqrt(jnp.mean(values * values, axis=-1, keepdims=True) + NORM_EPS) * gain


def rotate(values, positions):
    half_dim = values.shape[-1] // 2
    frequency = THETA_BASE ** (-jnp.arange(half_dim, dtype=jnp.float32) * 2.0 / values.shape[-1])
    angles = positions.astype(jnp.float32)[:, None] * frequency[None, :]
    cosine = jnp.cos(angles)[:, None, :]
    sine_part = jnp.sin(angles)[:, None, :]
    lower_half = values[..., :half_dim]
    upper_half = values[..., half_dim:]
    return jnp.concatenate(
        [
            lower_half * cosine - upper_half * sine_part,
            upper_half * cosine + lower_half * sine_part,
        ],
        axis=-1,
    )


def head_inputs(qk_raw, query_gain, key_gain, positions):
    row_count = qk_raw.shape[0]
    query_width = HEADS * HEAD_DIM
    query_heads = qk_raw[:, :query_width].reshape(row_count, HEADS, HEAD_DIM)
    key_heads = qk_raw[:, query_width:].reshape(row_count, KV_HEADS, HEAD_DIM)
    return (
        rotate(rms_norm(query_heads, query_gain), positions),
        rotate(rms_norm(key_heads, key_gain), positions),
    )


def swiglu(gateup):
    return jax.nn.silu(gateup[:, :FF]) * gateup[:, FF:]


def masked_scores(query_heads, key_heads, start_row):
    scores = jnp.einsum(
        "qgrd,kgd->grqk", query_heads, key_heads, preferred_element_type=jnp.float32
    ) * HEAD_DIM ** (-0.5)
    query_places = start_row + jnp.arange(query_heads.shape[0])
    allowed = jnp.arange(key_heads.shape[0])[None, :] <= query_places[:, None]
    return jnp.where(allowed, scores, MASK_FILL)


def forward_seq(seq_item):
    query_heads, key_heads, value_heads = seq_item
    length = query_heads.shape[0]
    block_rows = min(512, length)
    outputs = []
    log_parts = []
    for start_row in range(0, length, block_rows):
        stop_row = start_row + block_rows
        scores = masked_scores(query_heads[start_row:stop_row], key_heads[:stop_row], start_row)
        row_max = jnp.max(scores, axis=-1, keepdims=True)
        log_total = jnp.log(jnp.sum(jnp.exp(scores - row_max), axis=-1, keepdims=True)) + row_max
        attn_probs = jnp.exp(scores - log_total).astype(jnp.bfloat16)
        outputs.append(
            jnp.einsum(
                "grqk,kgd->qgrd",
                attn_probs,
                value_heads[:stop_row],
                preferred_element_type=jnp.float32,
            )
        )
        log_parts.append(log_total)
    return (jnp.concatenate(outputs, axis=0), jnp.concatenate(log_parts, axis=2))


def backward_seq(seq_item, staged):
    query_heads, key_heads, value_heads, log_totals, grad_att = seq_item
    length = query_heads.shape[0]
    block_rows = min(512, length)
    score_scale = HEAD_DIM ** (-0.5)
    grad_keys = jnp.zeros(key_heads.shape, jnp.float32)
    grad_values = jnp.zeros(value_heads.shape, jnp.float32)
    query_parts = []
    for start_row in range(0, length, block_rows):
        stop_row = start_row + block_rows
        scores = masked_scores(query_heads[start_row:stop_row], key_heads[:stop_row], start_row)
        attn_probs = jnp.exp(scores - log_totals[:, :, start_row:stop_row])
        grad_probs = jnp.einsum(
            "qgrd,kgd->grqk",
            grad_att[start_row:stop_row],
            value_heads[:stop_row],
            preferred_element_type=jnp.float32,
        )
        grad_values = grad_values.at[:stop_row].add(
            jnp.einsum(
                "grqk,qgrd->kgd",
                attn_probs.astype(jnp.bfloat16),
                grad_att[start_row:stop_row],
                preferred_element_type=jnp.float32,
            )
        )
        row_inner = jnp.sum(attn_probs * grad_probs, axis=-1, keepdims=True)
        grad_scores = (attn_probs * (grad_probs - row_inner)).astype(jnp.bfloat16)
        if staged is not None and start_row > 0:
            grad_scores = staged.advance(grad_scores)
        query_parts.append(
            jnp.einsum(
                "grqk,kgd->qgrd",
                grad_scores,
                key_heads[:stop_row],
                preferred_element_type=jnp.float32,
            )
            * score_scale
        )
        grad_keys = grad_keys.at[:stop_row].add(
            jnp.einsum(
                "grqk,qgrd->kgd",
                grad_scores,
                query_heads[start_row:stop_row],
                preferred_element_type=jnp.float32,
            )
            * score_scale
        )
        if staged is not None:
            grad_keys, grad_values, key_heads, query_parts[-1] = staged.advance(
                grad_keys, grad_values, key_heads, query_parts[-1]
            )
    return (jnp.concatenate(query_parts, axis=0), grad_keys, grad_values)


def adam_step(weight_now, grad_now, moment_one, moment_two, rate, decay):
    moment_one = BETA_ONE * moment_one + (1.0 - BETA_ONE) * grad_now
    moment_two = BETA_TWO * moment_two + (1.0 - BETA_TWO) * grad_now * grad_now
    corrected_one = moment_one / (1.0 - BETA_ONE**STEP)
    corrected_two = moment_two / (1.0 - BETA_TWO**STEP)
    weight_new = weight_now - rate * (
        corrected_one / (jnp.sqrt(corrected_two) + ADAM_EPS) + decay * weight_now
    )
    return (weight_new, moment_one, moment_two)


def local(
    tokens,
    cotangent,
    qkv_weight,
    out_weight,
    gateup_weight,
    down_weight,
    norm_gains,
    avg_qkv,
    avg_out,
    avg_gateup,
    avg_down,
    avg_gains,
    sq_qkv,
    sq_out,
    sq_gateup,
    sq_down,
    sq_gains,
):
    masters = (qkv_weight, out_weight, gateup_weight, down_weight, norm_gains)
    weights = gather_weights(masters)
    qkv_full, out_full, gateup_full, down_full, gain_full = weights
    gain_values = gain_full.astype(jnp.float32)
    norm_one = gain_values[:D]
    norm_two = gain_values[D : 2 * D]
    query_gain = gain_values[2 * D : 2 * D + HEAD_DIM]
    key_gain = gain_values[2 * D + HEAD_DIM :]
    row_count = tokens.shape[0]
    seq_count = row_count // LEN
    group_ratio = HEADS // KV_HEADS
    query_width = HEADS * HEAD_DIM
    key_width = KV_HEADS * HEAD_DIM
    positions = jnp.arange(row_count) % LEN
    inputs = tokens.astype(jnp.float32)
    hidden_one = rms_norm(inputs, norm_one).astype(jnp.bfloat16)
    packed = jnp.dot(hidden_one, qkv_full, preferred_element_type=jnp.float32)
    qk_raw = packed[:, : query_width + key_width]
    head_fn = partial(head_inputs, positions=positions)
    rotated_query, rotated_keys = head_fn(qk_raw, query_gain, key_gain)
    query_heads = rotated_query.astype(jnp.bfloat16).reshape(
        seq_count, LEN, KV_HEADS, group_ratio, HEAD_DIM
    )
    key_heads = rotated_keys.astype(jnp.bfloat16).reshape(seq_count, LEN, KV_HEADS, HEAD_DIM)
    value_heads = (
        packed[:, query_width + key_width :]
        .astype(jnp.bfloat16)
        .reshape(seq_count, LEN, KV_HEADS, HEAD_DIM)
    )
    attended, log_totals = lax.map(forward_seq, (query_heads, key_heads, value_heads))
    attended = attended.reshape(row_count, query_width).astype(jnp.bfloat16)
    branch = jnp.dot(attended, out_full, preferred_element_type=jnp.float32)
    middle = inputs + branch
    hidden_two = rms_norm(middle, norm_two).astype(jnp.bfloat16)
    gateup = jnp.dot(hidden_two, gateup_full, preferred_element_type=jnp.float32)
    activated = swiglu(gateup).astype(jnp.bfloat16)
    result = middle + jnp.dot(activated, down_full, preferred_element_type=jnp.float32)
    block_out = result.astype(jnp.bfloat16)
    qkv_back, out_back, gateup_back, down_back = weights[:4]
    grad_down = jnp.einsum("tf,td->fd", activated, cotangent, preferred_element_type=jnp.float32)
    grad_down = grad_down.astype(jnp.bfloat16)
    grad_act = jnp.einsum("td,fd->tf", cotangent, down_back, preferred_element_type=jnp.float32)
    unused_act, pullback = jax.vjp(swiglu, gateup)
    grad_gateup_raw = pullback(grad_act)[0].astype(jnp.bfloat16)
    grad_gateup = jnp.einsum(
        "td,tf->df", hidden_two, grad_gateup_raw, preferred_element_type=jnp.float32
    )
    grad_hidden2 = jnp.einsum(
        "tf,df->td", grad_gateup_raw, gateup_back, preferred_element_type=jnp.float32
    )
    grad_gateup = grad_gateup.astype(jnp.bfloat16)
    grad_hidden2, grad_down, grad_gateup = lax.optimization_barrier(
        (grad_hidden2, grad_down, grad_gateup)
    )
    staged = Staged(
        split_rows(jnp.split(grad_gateup, 3, axis=1) + jnp.split(grad_down, 2, axis=1)),
        (0, 1, 2, 0, 1),
    )
    unused_two, pullback = jax.vjp(rms_norm, middle, norm_two)
    grad_midpart, grad_norm2 = pullback(grad_hidden2)
    grad_middle = cotangent.astype(jnp.float32) + grad_midpart
    grad_branch = grad_middle.astype(jnp.bfloat16)
    grad_out = jnp.einsum("tq,td->qd", attended, grad_branch, preferred_element_type=jnp.float32)
    summed_out = reduce_matrix([grad_out.astype(jnp.bfloat16)], (2,))
    grad_att = jnp.einsum(
        "td,qd->tq", grad_branch, out_back, preferred_element_type=jnp.float32
    ).astype(jnp.bfloat16)
    grad_att = staged.advance(grad_att)
    grad_att = grad_att.reshape(seq_count, LEN, KV_HEADS, group_ratio, HEAD_DIM)
    by_seq = [
        backward_seq(
            tuple(
                item[seq] for item in (query_heads, key_heads, value_heads, log_totals, grad_att)
            ),
            staged if seq == 0 else None,
        )
        for seq in range(seq_count)
    ]
    grad_query, grad_keys, grad_values = (jnp.stack(part) for part in zip(*by_seq))
    finished = staged.finish()
    summed_gateup = gather_parts(finished[:3])
    summed_down = gather_parts(finished[3:])
    unused_heads, pullback = jax.vjp(head_fn, qk_raw, query_gain, key_gain)
    grad_qkraw, grad_qgain, grad_kgain = pullback(
        (
            grad_query.reshape(row_count, HEADS, HEAD_DIM),
            grad_keys.reshape(row_count, KV_HEADS, HEAD_DIM),
        )
    )
    grad_packed = jnp.concatenate(
        [grad_qkraw, grad_values.reshape(row_count, key_width)], axis=1
    ).astype(jnp.bfloat16)
    grad_qkv = jnp.einsum("td,tp->dp", hidden_one, grad_packed, preferred_element_type=jnp.float32)
    grad_hidden1 = jnp.einsum(
        "tp,dp->td", grad_packed, qkv_back, preferred_element_type=jnp.float32
    )
    unused_one, pullback = jax.vjp(rms_norm, inputs, norm_one)
    grad_inpart, grad_norm1 = pullback(grad_hidden1)
    grad_tokens = (grad_middle + grad_inpart).astype(jnp.bfloat16)
    grad_gains = jnp.concatenate([grad_norm1, grad_norm2, grad_qgain, grad_kgain], axis=0)
    summed_qkv = reduce_matrix(jnp.split(grad_qkv.astype(jnp.bfloat16), 2, axis=1), (1, 2))
    gain_rows = norm_gains.shape[0]
    all_gains = lax.psum(grad_gains, ("rep", "shard"))
    summed_gains = lax.dynamic_slice_in_dim(
        all_gains, lax.axis_index("shard") * gain_rows, gain_rows, axis=0
    )
    summed = (summed_qkv, summed_out, summed_gateup, summed_down, summed_gains)
    firsts = (avg_qkv, avg_out, avg_gateup, avg_down, avg_gains)
    seconds = (sq_qkv, sq_out, sq_gateup, sq_down, sq_gains)
    rates = (RATE_QKV, RATE_OUT, RATE_GATEUP, RATE_DOWN, GAIN_RATE)
    decays = (DECAY_RATE, DECAY_RATE, DECAY_RATE, DECAY_RATE, 0.0)
    new_weights = []
    new_firsts = []
    new_seconds = []
    for index_one in range(5):
        weight_new, moment_one, moment_two = adam_step(
            masters[index_one],
            summed[index_one],
            firsts[index_one],
            seconds[index_one],
            rates[index_one],
            decays[index_one],
        )
        new_weights.append(weight_new)
        new_firsts.append(moment_one)
        new_seconds.append(moment_two)
    return (
        (block_out, grad_tokens)
        + summed
        + tuple(new_weights)
        + tuple(new_firsts)
        + tuple(new_seconds)
    )


def solution(mesh):
    in_specs = (
        P(("rep", "shard"), None),
        P(("rep", "shard"), None),
        P("shard", None),
        P("shard", None),
        P("shard", None),
        P("shard", None),
        P("shard"),
        P("shard", None),
        P("shard", None),
        P("shard", None),
        P("shard", None),
        P("shard"),
        P("shard", None),
        P("shard", None),
        P("shard", None),
        P("shard", None),
        P("shard"),
    )
    out_specs = (
        P(("rep", "shard"), None),
        P(("rep", "shard"), None),
        P("shard", None),
        P("shard", None),
        P("shard", None),
        P("shard", None),
        P("shard"),
        P("shard", None),
        P("shard", None),
        P("shard", None),
        P("shard", None),
        P("shard"),
        P("shard", None),
        P("shard", None),
        P("shard", None),
        P("shard", None),
        P("shard"),
        P("shard", None),
        P("shard", None),
        P("shard", None),
        P("shard", None),
        P("shard"),
    )
    return jax.shard_map(local, mesh=mesh, in_specs=in_specs, out_specs=out_specs, check_vma=False)
```
